512 devices in a mesh: ctx: 128 (over y, z, core), head: 4 (over x).
Axes of the slice: x: 4, y: 4, z: 16, core: 2. Of those that a mesh axis runs over, the one named last changes fastest.
Arguments:
- queries: bfloat16 [32768, 2048], P('ctx', 'head'), may hold values from -16 to 16
- key_rows: bfloat16 [32768, 512], P('ctx', 'head'), may hold values from -16 to 16
- value_rows: bfloat16 [32768, 512], P('ctx', 'head'), may hold values from -6 to 6
- vertical_rows: int32 [8192, 4], P(None, 'head'), may hold values from 0 to 255, as said below
- slash_offsets: int32 [8, 4], P(None, 'head'), may hold values from 1 to 127
- block_mask: int32 [512, 2, 4], P('ctx', None, 'head'), may hold values 0 or 1
Outputs:
- attended: bfloat16 [32768, 2048], P(('ctx', 'head'))
The draws below stay inside these ranges and needn't reach their ends.
Inputs may be any that keep to these rules, and one draw needn't show every extreme that they name: `vertical_rows`: within each aligned block of 64 rows the entries of one column are distinct.
All inputs are finite; a program needn't handle non-finite values. No bound on the sum of `block_mask` on one device may be relied on, other than what follows from the above.
Results may differ from the reference program's by a relative error of at most 0.009.
Values may be sent and summed in bfloat16 or wider, within the bound.
A program may use at most 128 MiB of HBM per device.

```python
import jax
import jax.numpy as jnp
from jax import lax

HD = 128
QH = 16
KVH = 4
BLK = 64
VB = 64
NS = 8
TOK_DEV = 256
HALF = 128
TOKENS = 32768
LINES = 8192
N_CTX = 128


def draw_queries(key, part):
    key = jax.random.fold_in(key, 11)
    noise_part = jax.random.normal(key, (TOKENS, QH * HD), jnp.float32)
    return jnp.clip(noise_part, -16.0, 16.0).astype(jnp.bfloat16)


def draw_key_rows(key, part):
    key = jax.random.fold_in(key, 23)
    noise_part = jax.random.normal(key, (TOKENS, KVH * HD), jnp.float32)
    return jnp.clip(noise_part, -16.0, 16.0).astype(jnp.bfloat16)


def draw_vertical_rows(key, part):
    key = jax.random.fold_in(key, 37)
    ranks = jax.random.randint(key, (N_CTX, KVH, TOK_DEV), 0, 65536) * TOK_DEV + jnp.arange(TOK_DEV, dtype=jnp.int32)
    chosen = lax.top_k(ranks, VB)[1]
    return jnp.transpose(chosen, (0, 2, 1)).reshape(N_CTX * VB, KVH).astype(jnp.int32)


def with_ends(values, rng, smallest, high):
    place = [jax.random.randint(jax.random.fold_in(rng, axis), (), 0, length) for axis, length in enumerate(values.shape)]
    main_axis = values.shape.index(max(values.shape))
    neighbour = place[:main_axis] + [(place[main_axis] + 1) % values.shape[main_axis]] + place[main_axis + 1:]
    return values.at[tuple(place)].set(smallest).at[tuple(neighbour)].set(high)


def level_of(key, extent, pieces, smallest, top_value):
    level, own = 1.0, jax.random.fold_in(key, 6)
    for dim, shards_of in pieces:
        steps = jnp.exp(jax.random.uniform(jax.random.fold_in(own, dim), (shards_of,), jnp.float32, smallest / len(pieces), top_value / len(pieces)))
        level = level * jnp.repeat(steps, extent[dim] // shards_of).reshape([-1 if axis == dim else 1 for axis in range(len(extent))])
    return level


def scatter_about(stream_key, shape, width, bound, split=(), kind=jnp.bfloat16):
    values = width * jax.random.normal(stream_key, shape, jnp.float32)
    if split:
        values = values * level_of(stream_key, shape, split, -0.22, 0.18)
    return jnp.clip(values, -bound, bound).astype(kind)


def setup_inputs(seed: int = 0) -> dict:
    key_of = jax.random.split(jax.random.key(seed), 7)
    queries = draw_queries(jax.random.fold_in(key_of[6], 71), 0)
    key_rows = draw_key_rows(jax.random.fold_in(key_of[6], 71), 0)
    value_rows = scatter_about(key_of[2], (TOKENS, KVH * HD), 1.0, 6.0, ((0, 128), (1, 4)))
    vertical_rows = draw_vertical_rows(jax.random.fold_in(key_of[6], 71), 0)
    slash_offsets = with_ends(jax.random.randint(key_of[4], (NS, KVH), 1, HALF), jax.random.fold_in(key_of[4], 1), 1, HALF - 1).astype(jnp.int32)
    block_mask = with_ends((jax.random.randint(key_of[5], (TOKENS // BLK, HALF // BLK, KVH), 0, 2) < 1).astype(jnp.int32), jax.random.fold_in(key_of[5], 1), 0, 1)
    return {"queries": queries, "key_rows": key_rows, "value_rows": value_rows, "vertical_rows": vertical_rows, "slash_offsets": slash_offsets, "block_mask": block_mask}


def mirror_positions(row_ids):
    owner_ids = row_ids // TOK_DEV
    local_rows = row_ids % TOK_DEV
    half_index = jnp.where(local_rows < HALF, owner_ids, 2 * N_CTX - 1 - owner_ids)
    return (half_index * HALF + local_rows % HALF).astype(jnp.int32)


def local_allowed(positions, local_rows, mask_rows, slash):
    query_pos = positions[:, None]
    key_pos = positions[None, :]
    same_half = (query_pos // HALF) == (key_pos // HALF)
    causal = key_pos <= query_pos
    same_block = (query_pos // BLK) == (key_pos // BLK)
    offset = query_pos - key_pos
    slash_hit = jnp.any(offset[None, None] == jnp.transpose(slash)[:, :, None, None], axis=1)
    block_bits = mask_rows[local_rows // BLK][:, (positions % HALF) // BLK]
    block_hit = jnp.transpose(block_bits, (2, 0, 1)) == 1
    return same_half[None] & causal[None] & (same_block[None] | slash_hit | block_hit)


def reference(queries, key_rows, value_rows, vertical_rows, slash_offsets, block_mask):
    group_size = QH // KVH
    score_scale = HD ** -0.5
    all_pos = mirror_positions(jnp.arange(TOKENS, dtype=jnp.int32))
    owners = (jnp.arange(LINES, dtype=jnp.int32) // VB)[:, None]
    line_index = (owners * TOK_DEV + vertical_rows).astype(jnp.int32)
    head_ids = jnp.arange(KVH, dtype=jnp.int32)[None, :]
    key_tiles = key_rows.reshape(TOKENS, KVH, HD)
    value_tiles = value_rows.reshape(TOKENS, KVH, HD)
    line_keys = key_tiles[line_index, head_ids].astype(jnp.float32)
    line_values = value_tiles[line_index, head_ids].astype(jnp.float32)
    line_pos = all_pos[line_index]
    local_rows = jnp.arange(TOK_DEV, dtype=jnp.int32)

    def one_device(device):
        first_row = (device * TOK_DEV).astype(jnp.int32)
        query_tiles = lax.dynamic_slice_in_dim(queries, first_row, TOK_DEV, 0).astype(jnp.float32).reshape(TOK_DEV, KVH, group_size, HD)
        own_keys = lax.dynamic_slice_in_dim(key_tiles, first_row, TOK_DEV, 0).astype(jnp.float32)
        own_values = lax.dynamic_slice_in_dim(value_tiles, first_row, TOK_DEV, 0).astype(jnp.float32)
        positions = lax.dynamic_slice_in_dim(all_pos, first_row, TOK_DEV, 0)
        mask_rows = lax.dynamic_slice_in_dim(block_mask, (device * (TOK_DEV // BLK)).astype(jnp.int32), TOK_DEV // BLK, 0)
        allowed = local_allowed(positions, local_rows, mask_rows, slash_offsets)
        local_scores = jnp.einsum('tkgd,skd->kgts', query_tiles, own_keys) * score_scale
        local_scores = jnp.where(allowed[:, None], local_scores, -jnp.inf)
        line_scores = jnp.einsum('tkgd,nkd->kgtn', query_tiles, line_keys) * score_scale
        visible = jnp.transpose(line_pos)[:, None, :] < (positions - positions % HALF)[None, :, None]
        line_scores = jnp.where(visible[:, None], line_scores, -jnp.inf)
        peak = jnp.maximum(jnp.max(local_scores, axis=3), jnp.max(line_scores, axis=3))
        local_weights = jnp.exp(local_scores - peak[..., None])
        line_weights = jnp.exp(line_scores - peak[..., None])
        weight_sum = jnp.sum(local_weights, axis=3) + jnp.sum(line_weights, axis=3)
        numerator = jnp.einsum('kgts,skd->kgtd', local_weights, own_values) + jnp.einsum('kgtn,nkd->kgtd', line_weights, line_values)
        result = numerator / weight_sum[..., None]
        return jnp.transpose(result, (2, 0, 1, 3)).reshape(TOK_DEV, QH * HD).astype(jnp.bfloat16)

    blocks = lax.map(one_device, jnp.arange(N_CTX, dtype=jnp.int32))
    return blocks.reshape(TOKENS, QH * HD)
```

```python
import math

import jax
import jax.numpy as jnp
from jax import lax
from jax.experimental import pallas as pl
from jax.experimental.pallas import tpu as pltpu
from jax.sharding import PartitionSpec as P

HD = 128
BLK = 64
VB = 64
HALF = 128
NY = 4
NZ = 16
NC = 2
GROUP = 4
NEG = -1e30
SCALE = HD**-0.5 * math.log2(math.e)
MESH = pl.DeviceIdType.MESH


def kernel(
    q_hbm, k_hbm, v_hbm, vr_hbm, slash_ref, bm_ref, out_hbm,
    q_ref, k_ref, v_ref, vr_ref, lines, peak, acc, res,
    in_sem, y_send, y_recv, up_send, up_recv, dn_send, dn_recv,
    su_send, su_recv, sd_send, sd_recv, x_send, x_recv, own_sem,
):
    c = lax.axis_index("ctx")
    h = lax.axis_index("head")
    heads = lax.axis_size("head")
    y = c // (NZ * NC)
    z = (c // NC) % NZ
    core = c % NC

    def dev(yy, zz, cc):
        return (yy * (NZ * NC) + zz * NC + cc, h)

    sibling = dev(y, z, 1 - core)
    z_up = dev(y, (z + 1) % NZ, core)
    z_dn = dev(y, (z + NZ - 1) % NZ, core)

    loads = [
        pltpu.make_async_copy(src, dst, in_sem.at[i])
        for i, (src, dst) in enumerate(
            ((vr_hbm, vr_ref), (k_hbm, k_ref), (v_hbm, v_ref), (q_hbm, q_ref))
        )
    ]
    for load in loads:
        load.start()

    barrier = pltpu.get_barrier_semaphore()
    greeted = [sibling, z_up, z_dn]
    greeted += [dev((y + d) % NY, z, core) for d in (1, 2, 3)]
    greeted += [(c, (h + d) % heads) for d in (1, 2, 3)]
    for who in greeted:
        pl.semaphore_signal(barrier, inc=1, device_id=who, device_id_type=MESH)

    for load in loads[:3]:
        load.wait()
    chip_rows = vr_ref[y, pl.ds(z, 1), :]
    picks = lax.broadcasted_iota(jnp.int32, (2 * HALF, NC * VB), 0) == chip_rows
    picks = jnp.where(picks, 1.0, 0.0).astype(jnp.bfloat16)
    for kv, src in ((0, k_ref), (1, v_ref)):
        both = lax.dot_general(
            picks, src[...], (((0,), (0,)), ((), ())), preferred_element_type=jnp.float32
        ).astype(jnp.bfloat16)
        for cc in range(NC):
            @pl.when(core == cc)
            def _():
                lines[z, kv, y, cc] = both[cc * VB : (cc + 1) * VB]

    pl.semaphore_wait(barrier, len(greeted))

    def y_copy(d):
        block = lines.at[z, :, y, core]
        return pltpu.make_async_remote_copy(
            block, block, y_send.at[d - 1], y_recv.at[d - 1],
            device_id=dev((y + d) % NY, z, core), device_id_type=MESH,
        )

    for d in (1, 2, 3):
        y_copy(d).start()
    loads[3].wait()

    def z_copy(s, zz, upward):
        block = lines.at[zz, :, :, core]
        if upward:
            return pltpu.make_async_remote_copy(
                block, block, up_send.at[s], up_recv.at[s], device_id=z_up, device_id_type=MESH
            )
        return pltpu.make_async_remote_copy(
            block, block, dn_send.at[s], dn_recv.at[s], device_id=z_dn, device_id_type=MESH
        )

    def last_copy(zz, upward):
        kv = 0 if upward else 1
        block = lines.at[zz, kv, :, core]
        if upward:
            return pltpu.make_async_remote_copy(
                block, block, up_send.at[8], up_recv.at[8], device_id=z_up, device_id_type=MESH
            )
        return pltpu.make_async_remote_copy(
            block, block, dn_send.at[8], dn_recv.at[8], device_id=z_dn, device_id_type=MESH
        )

    def sib_copy(s, zz, upward, who):
        block = lines.at[zz, :, :, who]
        send, recv = (su_send, su_recv) if upward else (sd_send, sd_recv)
        return pltpu.make_async_remote_copy(
            block, block, send.at[s], recv.at[s], device_id=sibling, device_id_type=MESH
        )

    ones = jnp.ones((NY * NC * VB, HD), jnp.bfloat16)

    def queries_of(half):
        return jnp.concatenate(
            [
                q_ref[half * HALF : (half + 1) * HALF, g * HD : (g + 1) * HD]
                for g in range(GROUP)
            ],
            axis=0,
        )

    qi = lax.broadcasted_iota(jnp.int32, (HALF, HALF), 0)
    kj = lax.broadcasted_iota(jnp.int32, (HALF, HALF), 1)
    offset = qi - kj
    slash_hit = offset == slash_ref[0]
    for n in range(1, slash_ref.shape[0]):
        slash_hit = slash_hit | (offset == slash_ref[n])
    base = (qi // BLK == kj // BLK) | slash_hit
    for half in range(2):
        bits = [
            [jnp.full((HALF, HALF), bm_ref[kb, 2 * half + qb], jnp.int32) for kb in range(2)]
            for qb in range(2)
        ]
        top = jnp.where(kj < BLK, bits[0][0], bits[0][1])
        low = jnp.where(kj < BLK, bits[1][0], bits[1][1])
        hit = jnp.where(qi < BLK, top, low) == 1
        allowed = (kj <= qi) & (base | hit)
        bias = jnp.where(allowed, 0.0, NEG)
        rows = slice(half * HALF, (half + 1) * HALF)
        s = lax.dot_general(
            queries_of(half), k_ref[rows, :], (((1,), (1,)), ((), ())),
            preferred_element_type=jnp.float32,
        )
        s = s + jnp.concatenate([bias] * GROUP, axis=0)
        top_score = jnp.broadcast_to(jnp.max(s, axis=1, keepdims=True), s.shape)
        peak[half] = top_score
        weights = jnp.exp2((s - top_score) * SCALE).astype(jnp.bfloat16)
        vals = jnp.concatenate([v_ref[rows, :], ones[:HALF]], axis=1)
        acc[half] = jnp.dot(weights, vals, preferred_element_type=jnp.float32)

    lane = lax.broadcasted_iota(jnp.int32, (1, NC * VB), 1)

    def absorb(zz):
        low_bias, high_bias = [], []
        for yy in range(NY):
            is_low = vr_ref[yy, pl.ds(zz, 1), :] < HALF
            owner = yy * (NZ * NC) + zz * NC + lane // VB
            low_bias.append(jnp.where(is_low & (owner < c), 0.0, NEG))
            high_bias.append(jnp.where(is_low | (owner > c), 0.0, NEG))
        keys = lines[zz, 0].reshape(NY * NC * VB, HD)
        vals = jnp.concatenate([lines[zz, 1].reshape(NY * NC * VB, HD), ones], axis=1)
        for half, parts in ((0, low_bias), (1, high_bias)):
            bias = jnp.concatenate(parts, axis=1)
            s = lax.dot_general(
                queries_of(half), keys, (((1,), (1,)), ((), ())),
                preferred_element_type=jnp.float32,
            )
            s = s + bias
            old = peak[half]
            new = jnp.maximum(old, jnp.max(s, axis=1, keepdims=True))
            peak[half] = new
            weights = jnp.exp2((s - jnp.concatenate([new] * NY, axis=1)) * SCALE)
            rescale = jnp.exp2((old - new) * SCALE)
            acc[half] = acc[half] * jnp.concatenate([rescale] * 2, axis=1) + jnp.dot(
                weights.astype(jnp.bfloat16), vals, preferred_element_type=jnp.float32
            )

    for d in (1, 2, 3):
        y_copy(d).wait_recv()
    z_copy(1, z, True).start()
    z_copy(1, z, False).start()
    sib_copy(0, z, True, core).start()

    sib_copy(0, z, True, 1 - core).wait_recv()
    absorb(z)

    def step(s, carry):
        for upward in (True, False):
            zz = (z + NZ - s) % NZ if upward else (z + s) % NZ
            z_copy(s, zz, upward).wait_recv()
            @pl.when(s < 7)
            def _():
                z_copy(s + 1, zz, upward).start()
            @pl.when(s == 7)
            def _():
                last_copy(zz, upward).start()
            sib_copy(s, zz, upward, core).start()
            @pl.when(s > 1)
            def _():
                before = (z + NZ - s + 1) % NZ if upward else (z + s - 1) % NZ
                sib_copy(s - 1, before, upward, 1 - core).wait_recv()
                absorb(before)
        return carry

    lax.fori_loop(1, 8, step, 0)
    far = (z + 8) % NZ
    last_copy(far, True).wait_recv()
    last_copy(far, False).wait_recv()
    sib_copy(8, far, True, core).start()
    for upward in (True, False):
        before = (z + NZ - 7) % NZ if upward else (z + 7) % NZ
        sib_copy(7, before, upward, 1 - core).wait_recv()
        absorb(before)
    sib_copy(8, far, True, 1 - core).wait_recv()
    absorb(far)

    quarter = res.shape[0] // 4
    cols = GROUP * HD

    def x_copy(d):
        to = (h + d) % heads
        return pltpu.make_async_remote_copy(
            res.at[pl.ds(to * quarter, quarter), :],
            out_hbm.at[:, pl.ds(pl.multiple_of(h * cols, cols), cols)],
            x_send.at[d - 1], x_recv.at[d - 1],
            device_id=(c, to), device_id_type=MESH,
        )

    for half in range(2):
        total = acc[half]
        done = (total[:, :HD] / total[:, HD:]).astype(jnp.bfloat16)
        for g in range(GROUP):
            res[half * HALF : (half + 1) * HALF, g * HD : (g + 1) * HD] = done[
                g * HALF : (g + 1) * HALF
            ]
    own = pltpu.make_async_copy(
        res.at[pl.ds(h * quarter, quarter), :],
        out_hbm.at[:, pl.ds(pl.multiple_of(h * cols, cols), cols)],
        own_sem,
    )
    own.start()
    for d in (2, 1, 3):
        x_copy(d).start()

    for d in (1, 2, 3):
        y_copy(d).wait_send()
    sib_copy(0, z, True, core).wait_send()

    def drain(s, carry):
        for upward in (True, False):
            zz = (z + NZ - s) % NZ if upward else (z + s) % NZ
            z_copy(s, zz, upward).wait_send()
            sib_copy(s, zz, upward, core).wait_send()
        return carry

    lax.fori_loop(1, 8, drain, 0)
    last_copy(far, True).wait_send()
    last_copy(far, False).wait_send()
    sib_copy(8, far, True, core).wait_send()
    own.wait()
    for d in (1, 2, 3):
        x_copy(d).wait_send()
    for d in (1, 2, 3):
        x_copy(d).wait_recv()


def on_device(queries, key_rows, value_rows, vertical_rows, slash_offsets, block_mask):
    rows = queries.shape[0]
    heads = lax.axis_size("head")
    cols = queries.shape[1]
    dma = pltpu.SemaphoreType.DMA
    return pl.pallas_call(
        kernel,
        out_shape=jax.ShapeDtypeStruct((rows // heads, heads * cols), jnp.bfloat16),
        in_specs=[pl.BlockSpec(memory_space=pl.ANY)] * 4
        + [pl.BlockSpec(memory_space=pltpu.SMEM)] * 2,
        out_specs=pl.BlockSpec(memory_space=pl.ANY),
        scratch_shapes=[
            pltpu.VMEM((rows, cols), jnp.bfloat16),
            pltpu.VMEM((rows, HD), jnp.bfloat16),
            pltpu.VMEM((rows, HD), jnp.bfloat16),
            pltpu.VMEM((NY, NZ, NC * VB), jnp.int32),
            pltpu.VMEM((NZ, 2, NY, NC, VB, HD), jnp.bfloat16),
            pltpu.VMEM((2, GROUP * HALF, HD), jnp.float32),
            pltpu.VMEM((2, GROUP * HALF, 2 * HD), jnp.float32),
            pltpu.VMEM((rows, cols), jnp.bfloat16),
            dma((4,)),
            dma((3,)), dma((3,)),
            dma((9,)), dma((9,)), dma((9,)), dma((9,)),
            dma((9,)), dma((9,)), dma((9,)), dma((9,)),
            dma((3,)), dma((3,)),
            dma,
        ],
        compiler_params=pltpu.CompilerParams(
            collective_id=0, has_side_effects=True, vmem_limit_bytes=48 * 1024 * 1024
        ),
        cost_estimate=pl.CostEstimate(
            flops=4 * 1024 * 8192 * HD, bytes_accessed=2**20, transcendentals=1024 * 8192
        ),
    )(
        queries, key_rows, value_rows,
        vertical_rows.reshape(NY, NZ, NC * VB),
        slash_offsets.reshape(-1),
        jnp.transpose(block_mask, (1, 2, 0)).reshape(2, -1),
    )


def solution(mesh):
    placed = (
        P("ctx", "head"),
        P("ctx", "head"),
        P("ctx", "head"),
        P(None, "head"),
        P(None, "head"),
        P("ctx", None, "head"),
    )
    return jax.shard_map(
        on_device, mesh=mesh, in_specs=placed, out_specs=P(("ctx", "head"), None), check_vma=False
    )
```

```python
import math

import jax
import jax.numpy as jnp
from jax import lax
from jax.experimental import pallas as pl
from jax.experimental.pallas import tpu as pltpu
from jax.sharding import PartitionSpec as P

HD = 128
BLK = 64
VB = 64
HALF = 128
NY = 4
NZ = 16
NC = 2
GROUP = 4
NEG = -1e30
SCALE = HD**-0.5 * math.log2(math.e)
MESH = pl.DeviceIdType.MESH


TREE = {0: ((4, 4), (1, 1)), 1: ((1, 2),), 2: ((1, 3),), 4: ((2, 6), (1, 5)), 6: ((2, 8), (1, 7))}
ORDER = (0, -1, 1, -4, 4, -2, 2, -5, 5, -6, 6, -3, 3, -7, 7, 8)
STEPS = {
    0: (("own", 2), ("rest", 1)),
    1: (("own", 5), ("own", 6)),
    2: (("rest", 4), ("own", 3)),
    4: (("rest", 2), ("own", 7), ("own", 8)),
    6: (("rest", 5),),
    7: (("rest", 6),),
    9: (("rest", 3),),
    11: (("rest", 7), ("rest", 8)),
}
ROWS = 2 * VB
SPLIT = 48


def kernel(
    q_hbm, k_hbm, v_hbm, vr_hbm, slash_ref, bm_ref, out_hbm,
    q_ref, k_ref, v_ref, vr_ref, lines, peak, acc, res,
    in_sem, a_send, a_recv, b_send, b_recv, y_send, y_recv,
    s_send, s_recv, x_send, x_recv, own_sem,
):
    c = lax.axis_index("ctx")
    h = lax.axis_index("head")
    heads = lax.axis_size("head")
    y = c // (NZ * NC)
    z = (c // NC) % NZ
    core = c % NC

    def dev(yy, zz, cc):
        return (yy * (NZ * NC) + zz * NC + cc, h)

    sibling = dev(y, z, 1 - core)
    opposite = (y + 2) % NY

    def along(hop, upward):
        return (z + hop) % NZ if upward else (z + NZ - hop) % NZ

    def owner_of(distance, upward):
        return along(distance, not upward)

    loads = [
        pltpu.make_async_copy(src, dst, in_sem.at[i])
        for i, (src, dst) in enumerate(
            ((vr_hbm, vr_ref), (k_hbm, k_ref), (v_hbm, v_ref), (q_hbm, q_ref))
        )
    ]
    for load in loads:
        load.start()

    barrier = pltpu.get_barrier_semaphore()
    greeted = [sibling]
    greeted += [dev(y, along(hop, up), core) for hop in (1, 2, 4) for up in (True, False)]
    greeted += [dev((y + d) % NY, z, core) for d in (1, 2, 3)]
    greeted += [(c, (h + d) % heads) for d in (1, 2, 3)]
    for who in greeted:
        pl.semaphore_signal(barrier, inc=1, device_id=who, device_id_type=MESH)

    for load in loads[:3]:
        load.wait()
    chip_rows = vr_ref[y, pl.ds(z, 1), :]
    picks = lax.broadcasted_iota(jnp.int32, (2 * HALF, NC * VB), 0) == chip_rows
    picks = jnp.where(picks, 1.0, 0.0).astype(jnp.bfloat16)
    for kv, src in ((0, k_ref), (1, v_ref)):
        both = lax.dot_general(
            picks, src[...], (((0,), (0,)), ((), ())), preferred_element_type=jnp.float32
        ).astype(jnp.bfloat16)
        for cc in range(NC):
            @pl.when(core == cc)
            def _():
                lines[z, y, cc, kv * VB : (kv + 1) * VB] = both[cc * VB : (cc + 1) * VB]

    pl.semaphore_wait(barrier, len(greeted))

    def remote(block, send, recv, to):
        return pltpu.make_async_remote_copy(
            block, block, send, recv, device_id=to, device_id_type=MESH
        )

    def z_copy(kind, held, hop, reached, upward):
        zz = owner_of(held, upward)
        send, recv, yy, first = (
            (a_send, a_recv, y, 0) if kind == "own" else (b_send, b_recv, opposite, SPLIT)
        )
        cut = 64 if kind == "own" else 96
        last = ROWS
        if reached == 8:
            first, last = (first, cut) if upward else (cut, ROWS)
        return remote(
            lines.at[zz, yy, core, pl.ds(first, last - first)],
            send.at[int(upward), reached], recv.at[int(upward), reached],
            dev(y, along(hop, upward), core),
        )

    def z_sends(kind, held):
        return [
            z_copy(kind, held, hop, reached, upward)
            for hop, reached in TREE.get(held, ())
            for upward in (True, False)
        ]

    def z_arrivals(kind, reached):
        hop, held = next(
            (hop, held) for held, to in TREE.items() for hop, at in to if at == reached
        )
        return [z_copy(kind, held, hop, reached, upward) for upward in (True, False)]

    def y_copy(distance, d):
        rows = SPLIT if d == 2 and distance != 0 else ROWS
        return remote(
            lines.at[(z + NZ + distance) % NZ, y, core, pl.ds(0, rows)],
            y_send.at[d - 1, distance % NZ], y_recv.at[d - 1, distance % NZ],
            dev((y + d) % NY, z, core),
        )

    def s_copy(rel):
        return remote(
            lines.at[(z + rel) % NZ, :, core], s_send.at[rel], s_recv.at[rel], sibling
        )

    def signed(distance):
        return (0,) if distance == 0 else (8,) if distance == 8 else (-distance, distance)

    def own_step(distance):
        for copy in z_arrivals("own", distance):
            copy.wait_recv()
        for copy in z_sends("own", distance):
            copy.start()
        for at in signed(distance):
            for d in (2, 1, 3):
                y_copy(at, d).start()

    def rest_step(distance):
        for copy in z_arrivals("rest", distance):
            copy.wait_recv()
        for copy in z_sends("rest", distance):
            copy.start()
        for at in signed(distance):
            for d in (1, 2, 3):
                y_copy(at, d).wait_recv()
            s_copy(at % NZ).start()

    for copy in z_sends("own", 0):
        copy.start()
    for d in (2, 1, 3):
        y_copy(0, d).start()
    loads[3].wait()

    ones = jnp.ones((NY * NC * VB, HD), jnp.bfloat16)

    def queries_of(half):
        return jnp.concatenate(
            [
                q_ref[half * HALF : (half + 1) * HALF, g * HD : (g + 1) * HD]
                for g in range(GROUP)
            ],
            axis=0,
        )

    qi = lax.broadcasted_iota(jnp.int32, (HALF, HALF), 0)
    kj = lax.broadcasted_iota(jnp.int32, (HALF, HALF), 1)
    offset = qi - kj
    slash_hit = offset == slash_ref[0]
    for n in range(1, slash_ref.shape[0]):
        slash_hit = slash_hit | (offset == slash_ref[n])
    base = (qi // BLK == kj // BLK) | slash_hit
    for half in range(2):
        bits = [
            [jnp.full((HALF, HALF), bm_ref[kb, 2 * half + qb], jnp.int32) for kb in range(2)]
            for qb in range(2)
        ]
        top = jnp.where(kj < BLK, bits[0][0], bits[0][1])
        low = jnp.where(kj < BLK, bits[1][0], bits[1][1])
        hit = jnp.where(qi < BLK, top, low) == 1
        allowed = (kj <= qi) & (base | hit)
        bias = jnp.where(allowed, 0.0, NEG)
        rows = slice(half * HALF, (half + 1) * HALF)
        s = lax.dot_general(
            queries_of(half), k_ref[rows, :], (((1,), (1,)), ((), ())),
            preferred_element_type=jnp.float32,
        )
        s = s + jnp.concatenate([bias] * GROUP, axis=0)
        top_score = jnp.broadcast_to(jnp.max(s, axis=1, keepdims=True), s.shape)
        peak[half] = top_score
        weights = jnp.exp2((s - top_score) * SCALE).astype(jnp.bfloat16)
        vals = jnp.concatenate([v_ref[rows, :], ones[:HALF]], axis=1)
        acc[half] = jnp.dot(weights, vals, preferred_element_type=jnp.float32)

    lane = lax.broadcasted_iota(jnp.int32, (1, NC * VB), 1)

    def absorb(zz):
        low_bias, high_bias = [], []
        for yy in range(NY):
            is_low = vr_ref[yy, pl.ds(zz, 1), :] < HALF
            owner = yy * (NZ * NC) + zz * NC + lane // VB
            low_bias.append(jnp.where(is_low & (owner < c), 0.0, NEG))
            high_bias.append(jnp.where(is_low | (owner > c), 0.0, NEG))
        keys = lines[zz, :, :, :VB].reshape(NY * NC * VB, HD)
        vals = jnp.concatenate([lines[zz, :, :, VB:].reshape(NY * NC * VB, HD), ones], axis=1)
        for half, parts in ((0, low_bias), (1, high_bias)):
            bias = jnp.concatenate(parts, axis=1)
            s = lax.dot_general(
                queries_of(half), keys, (((1,), (1,)), ((), ())),
                preferred_element_type=jnp.float32,
            )
            s = s + bias
            old = peak[half]
            new = jnp.maximum(old, jnp.max(s, axis=1, keepdims=True))
            peak[half] = new
            weights = jnp.exp2((s - jnp.concatenate([new] * NY, axis=1)) * SCALE)
            rescale = jnp.exp2((old - new) * SCALE)
            acc[half] = acc[half] * jnp.concatenate([rescale] * 2, axis=1) + jnp.dot(
                weights.astype(jnp.bfloat16), vals, preferred_element_type=jnp.float32
            )

    own_step(1)
    for d in (2, 1, 3):
        y_copy(0, d).wait_recv()
    for copy in z_sends("rest", 0):
        copy.start()
    s_copy(0).start()
    own_step(4)

    def chunk(i, carry):
        for j, todo in STEPS.items():
            @pl.when(i == j)
            def _():
                for kind, distance in todo:
                    (own_step if kind == "own" else rest_step)(distance)
        rel = jnp.int32(0)
        for j, distance in enumerate(ORDER):
            rel = jnp.where(i == j, distance % NZ, rel)
        s_copy(rel).wait_recv()
        absorb((z + rel) % NZ)
        return carry

    lax.fori_loop(0, NZ, chunk, 0)

    quarter = res.shape[0] // 4
    cols = GROUP * HD

    def x_copy(d):
        to = (h + d) % heads
        return pltpu.make_async_remote_copy(
            res.at[pl.ds(to * quarter, quarter), :],
            out_hbm.at[:, pl.ds(pl.multiple_of(h * cols, cols), cols)],
            x_send.at[d - 1], x_recv.at[d - 1],
            device_id=(c, to), device_id_type=MESH,
        )

    for half in range(2):
        total = acc[half]
        done = (total[:, :HD] / total[:, HD:]).astype(jnp.bfloat16)
        for g in range(GROUP):
            res[half * HALF : (half + 1) * HALF, g * HD : (g + 1) * HD] = done[
                g * HALF : (g + 1) * HALF
            ]
    own = pltpu.make_async_copy(
        res.at[pl.ds(h * quarter, quarter), :],
        out_hbm.at[:, pl.ds(pl.multiple_of(h * cols, cols), cols)],
        own_sem,
    )
    own.start()
    for d in (2, 1, 3):
        x_copy(d).start()

    for kind in ("own", "rest"):
        for held in TREE:
            for copy in z_sends(kind, held):
                copy.wait_send()
    for distance in ORDER:
        for d in (1, 2, 3):
            y_copy(distance, d).wait_send()

    def drain(rel, carry):
        s_copy(rel).wait_send()
        return carry

    lax.fori_loop(0, NZ, drain, 0)
    own.wait()
    for d in (1, 2, 3):
        x_copy(d).wait_send()
    for d in (1, 2, 3):
        x_copy(d).wait_recv()


def on_device(queries, key_rows, value_rows, vertical_rows, slash_offsets, block_mask):
    rows = queries.shape[0]
    heads = lax.axis_size("head")
    cols = queries.shape[1]
    dma = pltpu.SemaphoreType.DMA
    return pl.pallas_call(
        kernel,
        out_shape=jax.ShapeDtypeStruct((rows // heads, heads * cols), jnp.bfloat16),
        in_specs=[pl.BlockSpec(memory_space=pltpu.HBM)] * 4
        + [pl.BlockSpec(memory_space=pltpu.SMEM)] * 2,
        out_specs=pl.BlockSpec(memory_space=pl.ANY),
        scratch_shapes=[
            pltpu.VMEM((rows, cols), jnp.bfloat16),
            pltpu.VMEM((rows, HD), jnp.bfloat16),
            pltpu.VMEM((rows, HD), jnp.bfloat16),
            pltpu.VMEM((NY, NZ, NC * VB), jnp.int32),
            pltpu.VMEM((NZ, NY, NC, ROWS, HD), jnp.bfloat16),
            pltpu.VMEM((2, GROUP * HALF, HD), jnp.float32),
            pltpu.VMEM((2, GROUP * HALF, 2 * HD), jnp.float32),
            pltpu.VMEM((rows, cols), jnp.bfloat16),
            dma((4,)),
            dma((2, 9)), dma((2, 9)), dma((2, 9)), dma((2, 9)),
            dma((3, NZ)), dma((3, NZ)),
            dma((NZ,)), dma((NZ,)),
            dma((3,)), dma((3,)),
            dma,
        ],
        compiler_params=pltpu.CompilerParams(
            collective_id=0, has_side_effects=True, vmem_limit_bytes=60 * 1024 * 1024
        ),
        cost_estimate=pl.CostEstimate(
            flops=4 * 1024 * 8192 * HD, bytes_accessed=2**20, transcendentals=1024 * 8192
        ),
    )(
        queries, key_rows, value_rows,
        vertical_rows.reshape(NY, NZ, NC * VB),
        slash_offsets.reshape(-1),
        jnp.transpose(block_mask, (1, 2, 0)).reshape(2, -1),
    )


def solution(mesh):
    placed = (
        P("ctx", "head"),
        P("ctx", "head"),
        P("ctx", "head"),
        P(None, "head"),
        P(None, "head"),
        P("ctx", None, "head"),
    )
    return jax.shard_map(
        on_device, mesh=mesh, in_specs=placed, out_specs=P(("ctx", "head"), None), check_vma=False
    )
```

```python
import math

import jax
import jax.numpy as jnp
from jax import lax
from jax.experimental import pallas as pl
from jax.experimental.pallas import tpu as pltpu
from jax.sharding import PartitionSpec as P

HD = 128
BLK = 64
VB = 64
HALF = 128
NY = 4
NZ = 16
NC = 2
GROUP = 4
NEG = -1e30
SCALE = HD**-0.5 * math.log2(math.e)
MESH = pl.DeviceIdType.MESH


TREE = {0: ((2, 2), (1, 1)), 2: ((2, 4), (1, 3)), 4: ((2, 6), (1, 5)), 6: ((2, 8), (1, 7))}
HOPS = (2, 1)
PAIRS = (1, 2, 3, 4, 5, 6)
LAST = 7
FIRST = (("own", 1), ("own", 2), ("first", 0))
EARLY = (("rest", 1), ("own", 4), ("own", 3), ("rest", 2))
STEPS = {
    1: (("own", 6), ("own", 5)),
    2: (("rest", 4),),
    3: (("rest", 3),),
    4: (("own", 8), ("own", 7)),
    5: (("rest", 6),),
    6: (("rest", 5),),
    8: (("rest", 8),),
    9: (("rest", 7),),
}
ROWS = 2 * VB
SPLIT = 32


def kernel(
    q_hbm, k_hbm, v_hbm, vr_hbm, slash_ref, bm_ref, out_hbm,
    q_ref, k_ref, v_ref, vr_ref, lines, bias_ref, peak, acc, res,
    in_sem, a_send, a_recv, b_send, b_recv, y_send, y_recv,
    s_send, s_recv, x_send, x_recv, own_sem,
):
    c = lax.axis_index("ctx")
    h = lax.axis_index("head")
    heads = lax.axis_size("head")
    y = c // (NZ * NC)
    z = (c // NC) % NZ
    core = c % NC

    def dev(yy, zz, cc):
        return (yy * (NZ * NC) + zz * NC + cc, h)

    sibling = dev(y, z, 1 - core)
    opposite = (y + 2) % NY

    def along(hop, upward):
        return (z + hop) % NZ if upward else (z + NZ - hop) % NZ

    def owner_of(distance, upward):
        return along(distance, not upward)

    loads = [
        pltpu.make_async_copy(src, dst, in_sem.at[i])
        for i, (src, dst) in enumerate(
            [(vr_hbm, vr_ref), (k_hbm, k_ref), (v_hbm, v_ref)]
            + [
                (
                    q_hbm.at[pl.ds(half * HALF, HALF), pl.ds(g * HD, HD)],
                    q_ref.at[half * GROUP + g],
                )
                for half in range(2)
                for g in range(GROUP)
            ]
        )
    ]
    for load in loads:
        load.start()

    barrier = pltpu.get_barrier_semaphore()
    greeted = [dev(y, along(hop, up), core) for hop in HOPS for up in (True, False)]
    greeted += [dev((y + d) % NY, z, core) for d in (1, 2, 3)]
    greeted += [(c, (h + d) % heads) for d in (1, 2, 3)]
    greeted += [sibling]
    for who in greeted:
        pl.semaphore_signal(barrier, inc=1, device_id=who, device_id_type=MESH)

    for load in loads[:3]:
        load.wait()
    chip_rows = vr_ref[y, pl.ds(z, 1), :]
    picks = lax.broadcasted_iota(jnp.int32, (2 * HALF, NC * VB), 0) == chip_rows
    picks = jnp.where(picks, 1.0, 0.0).astype(jnp.bfloat16)
    for kv, src in ((0, k_ref), (1, v_ref)):
        both = lax.dot_general(
            picks, src[...], (((0,), (0,)), ((), ())), preferred_element_type=jnp.float32
        ).astype(jnp.bfloat16)
        for cc in range(NC):
            @pl.when(core == cc)
            def _():
                lines[z, y, cc, kv * VB : (kv + 1) * VB] = both[cc * VB : (cc + 1) * VB]

    pl.semaphore_wait(barrier, len(greeted))

    def remote(block, send, recv, to):
        return pltpu.make_async_remote_copy(
            block, block, send, recv, device_id=to, device_id_type=MESH
        )

    def z_copy(kind, held, hop, reached, upward):
        zz = owner_of(held, upward)
        send, recv, yy, first = (
            (a_send, a_recv, y, 0) if kind == "own" else (b_send, b_recv, opposite, SPLIT)
        )
        cut = 64 if kind == "own" else 96
        last = ROWS
        if reached == 8:
            first, last = (first, cut) if upward else (cut, ROWS)
        return remote(
            lines.at[zz, yy, core, pl.ds(first, last - first)],
            send.at[int(upward), reached], recv.at[int(upward), reached],
            dev(y, along(hop, upward), core),
        )

    def z_sends(kind, held):
        return [
            z_copy(kind, held, hop, reached, upward)
            for hop, reached in TREE.get(held, ())
            for upward in (True, False)
        ]

    def z_arrivals(kind, reached):
        hop, held = next(
            (hop, held) for held, to in TREE.items() for hop, at in to if at == reached
        )
        return [z_copy(kind, held, hop, reached, upward) for upward in (True, False)]

    def y_copy(distance, d):
        rows = SPLIT if d == 2 and distance != 0 else ROWS
        return remote(
            lines.at[(z + NZ + distance) % NZ, y, core, pl.ds(0, rows)],
            y_send.at[d - 1, distance % NZ], y_recv.at[d - 1, distance % NZ],
            dev((y + d) % NY, z, core),
        )

    def s_copy(rel):
        return remote(
            lines.at[(z + rel) % NZ, :, core], s_send.at[rel], s_recv.at[rel], sibling
        )

    def signed(distance):
        return (0,) if distance == 0 else (8,) if distance == 8 else (-distance, distance)

    def own_step(distance):
        for copy in z_arrivals("own", distance):
            copy.wait_recv()
        for copy in z_sends("own", distance):
            copy.start()
        for at in signed(distance):
            for d in (2, 1, 3):
                y_copy(at, d).start()

    def rest_step(distance):
        for copy in z_arrivals("rest", distance):
            copy.wait_recv()
        for copy in z_sends("rest", distance):
            copy.start()
        for at in signed(distance):
            for d in (1, 2, 3):
                y_copy(at, d).wait_recv()
            s_copy(at % NZ).start()

    for copy in z_sends("own", 0):
        copy.start()
    for d in (2, 1, 3):
        y_copy(0, d).start()

    ones = jnp.ones((NY * NC * VB, HD), jnp.bfloat16)

    owner = (
        lax.broadcasted_iota(jnp.int32, (NZ, NC * VB), 0) * NC
        + lax.broadcasted_iota(jnp.int32, (NZ, NC * VB), 1) // VB
    )
    for yy in range(NY):
        is_low = vr_ref[yy] < HALF
        at = slice(yy * NC * VB, (yy + 1) * NC * VB)
        before = owner + yy * (NZ * NC) < c
        after = owner + yy * (NZ * NC) > c
        bias_ref[0, :, at] = jnp.where(is_low & before, 0.0, NEG)
        bias_ref[1, :, at] = jnp.where(is_low | after, 0.0, NEG)

    for load in loads[3:]:
        load.wait()

    qi = lax.broadcasted_iota(jnp.int32, (HALF, HALF), 0)
    kj = lax.broadcasted_iota(jnp.int32, (HALF, HALF), 1)
    offset = qi - kj
    slash_hit = offset == slash_ref[0]
    for n in range(1, slash_ref.shape[0]):
        slash_hit = slash_hit | (offset == slash_ref[n])
    base = (qi // BLK == kj // BLK) | slash_hit
    for half in range(2):
        bits = [
            [jnp.full((HALF, HALF), bm_ref[kb, 2 * half + qb], jnp.int32) for kb in range(2)]
            for qb in range(2)
        ]
        top = jnp.where(kj < BLK, bits[0][0], bits[0][1])
        low = jnp.where(kj < BLK, bits[1][0], bits[1][1])
        hit = jnp.where(qi < BLK, top, low) == 1
        allowed = (kj <= qi) & (base | hit)
        bias = jnp.where(allowed, 0.0, NEG)
        rows = slice(half * HALF, (half + 1) * HALF)
        vals = jnp.concatenate([v_ref[rows, :], ones[:HALF]], axis=1)
        for t in range(half * GROUP, (half + 1) * GROUP):
            s = lax.dot_general(
                q_ref[t], k_ref[rows, :], (((1,), (1,)), ((), ())),
                preferred_element_type=jnp.float32,
            )
            s = s + bias
            top_score = jnp.broadcast_to(jnp.max(s, axis=1, keepdims=True), s.shape)
            peak[t] = top_score
            weights = jnp.exp2((s - top_score) * SCALE).astype(jnp.bfloat16)
            acc[t] = jnp.dot(weights, vals, preferred_element_type=jnp.float32)

    def absorb(half, chunks):
        def all_keys(first):
            return jnp.concatenate(
                [lines[zz, :, :, first : first + VB].reshape(NY * NC * VB, HD) for zz in chunks],
                axis=0,
            )

        keys = all_keys(0)
        vals = jnp.concatenate(
            [all_keys(VB), jnp.concatenate([ones] * len(chunks), axis=0)], axis=1
        )
        bias = jnp.concatenate([bias_ref[half, pl.ds(zz, 1), :] for zz in chunks], axis=1)
        scores = [
            lax.dot_general(
                q_ref[half * GROUP + g], keys, (((1,), (1,)), ((), ())),
                preferred_element_type=jnp.float32,
            )
            + bias
            for g in range(GROUP)
        ]
        for g in range(GROUP):
            t = half * GROUP + g
            s = scores[g]
            old = peak[t]
            new = jnp.maximum(old, jnp.max(s, axis=1, keepdims=True))
            peak[t] = new
            weights = jnp.exp2((s - jnp.concatenate([new] * (NY * len(chunks)), axis=1)) * SCALE)
            rescale = jnp.exp2((old - new) * SCALE)
            acc[t] = acc[t] * jnp.concatenate([rescale] * 2, axis=1) + jnp.dot(
                weights.astype(jnp.bfloat16), vals, preferred_element_type=jnp.float32
            )

    def first_step(distance):
        for d in (2, 1, 3):
            y_copy(distance, d).wait_recv()
        for copy in z_sends("rest", distance):
            copy.start()
        s_copy(distance).start()

    def do(todo):
        for kind, distance in todo:
            {"own": own_step, "rest": rest_step, "first": first_step}[kind](distance)

    do(FIRST)

    def near(half, carry):
        absorb(half, [z])
        return carry

    s_copy(0).wait_recv()
    lax.fori_loop(0, 2, near, 0)

    do(EARLY)

    def pair(u, carry):
        half = u % 2
        for j, todo in STEPS.items():
            @pl.when(u == j)
            def _():
                do(todo)
        distance = jnp.int32(0)
        for j, at in enumerate(PAIRS):
            distance = jnp.where(u // 2 == j, at, distance)

        @pl.when(half == 0)
        def _():
            s_copy(NZ - distance).wait_recv()
            s_copy(distance).wait_recv()

        chunks = [(z + NZ - distance) % NZ, (z + distance) % NZ]

        @pl.when((half == 1) | (jnp.minimum(chunks[0], chunks[1]) * NC < c))
        def _():
            absorb(half, chunks)
        return carry

    lax.fori_loop(0, 2 * len(PAIRS), pair, 0)
    for rel in (NZ - LAST, LAST, 8):
        s_copy(rel).wait_recv()

    quarter = res.shape[0] // 4
    cols = GROUP * HD

    def x_copy(to, whose):
        return pltpu.make_async_remote_copy(
            res.at[pl.ds(to * quarter, quarter), :],
            out_hbm.at[:, pl.ds(pl.multiple_of(h * cols, cols), cols)],
            x_send.at[to], x_recv.at[whose],
            device_id=(c, to), device_id_type=MESH,
        )

    own = pltpu.make_async_copy(
        res.at[pl.ds(h * quarter, quarter), :],
        out_hbm.at[:, pl.ds(pl.multiple_of(h * cols, cols), cols)],
        own_sem,
    )

    def finish(half, carry):
        absorb(half, [(z + rel) % NZ for rel in (NZ - LAST, LAST, 8)])
        rows = pl.ds(pl.multiple_of(half * HALF, HALF), HALF)
        for g in range(GROUP):
            total = acc[half * GROUP + g]
            res[rows, g * HD : (g + 1) * HD] = (total[:, :HD] / total[:, HD:]).astype(jnp.bfloat16)
        for part in range(2):
            to = half * 2 + part
            @pl.when(to == h)
            def _():
                own.start()
            @pl.when(to != h)
            def _():
                x_copy(to, h).start()
        return carry

    lax.fori_loop(0, 2, finish, 0)

    for kind in ("own", "rest"):
        for held in TREE:
            for copy in z_sends(kind, held):
                copy.wait_send()
    for distance in range(NZ):
        for d in (1, 2, 3):
            y_copy(distance, d).wait_send()

    def drain(rel, carry):
        s_copy(rel).wait_send()
        return carry

    lax.fori_loop(0, NZ, drain, 0)
    own.wait()
    for to in range(4):
        @pl.when(to != h)
        def _():
            x_copy(to, to).wait_send()
            x_copy(to, to).wait_recv()


def on_device(queries, key_rows, value_rows, vertical_rows, slash_offsets, block_mask):
    rows = queries.shape[0]
    heads = lax.axis_size("head")
    cols = queries.shape[1]
    dma = pltpu.SemaphoreType.DMA
    return pl.pallas_call(
        kernel,
        out_shape=jax.ShapeDtypeStruct((rows // heads, heads * cols), jnp.bfloat16),
        in_specs=[pl.BlockSpec(memory_space=pltpu.HBM)] * 4
        + [pl.BlockSpec(memory_space=pltpu.SMEM)] * 2,
        out_specs=pl.BlockSpec(memory_space=pl.ANY),
        scratch_shapes=[
            pltpu.VMEM((2 * GROUP, HALF, HD), jnp.bfloat16),
            pltpu.VMEM((rows, HD), jnp.bfloat16),
            pltpu.VMEM((rows, HD), jnp.bfloat16),
            pltpu.VMEM((NY, NZ, NC * VB), jnp.int32),
            pltpu.VMEM((NZ, NY, NC, ROWS, HD), jnp.bfloat16),
            pltpu.VMEM((2, NZ, NY * NC * VB), jnp.float32),
            pltpu.VMEM((2 * GROUP, HALF, HD), jnp.float32),
            pltpu.VMEM((2 * GROUP, HALF, 2 * HD), jnp.float32),
            pltpu.VMEM((rows, cols), jnp.bfloat16),
            dma((3 + 2 * GROUP,)),
            dma((2, 9)), dma((2, 9)), dma((2, 9)), dma((2, 9)),
            dma((3, NZ)), dma((3, NZ)),
            dma((NZ,)), dma((NZ,)),
            dma((4,)), dma((4,)),
            dma,
        ],
        compiler_params=pltpu.CompilerParams(
            collective_id=0, has_side_effects=True, vmem_limit_bytes=60 * 1024 * 1024
        ),
        cost_estimate=pl.CostEstimate(
            flops=4 * 1024 * 8192 * HD, bytes_accessed=2**20, transcendentals=1024 * 8192
        ),
    )(
        queries, key_rows, value_rows,
        vertical_rows.reshape(NY, NZ, NC * VB),
        slash_offsets.reshape(-1),
        jnp.transpose(block_mask, (1, 2, 0)).reshape(2, -1),
    )


def solution(mesh):
    placed = (
        P("ctx", "head"),
        P("ctx", "head"),
        P("ctx", "head"),
        P(None, "head"),
        P(None, "head"),
        P("ctx", None, "head"),
    )
    return jax.shard_map(
        on_device, mesh=mesh, in_specs=placed, out_specs=P(("ctx", "head"), None), check_vma=False
    )
```

```python
import math

import jax
import jax.numpy as jnp
from jax import lax
from jax.experimental import pallas as pl
from jax.experimental.pallas import tpu as pltpu
from jax.sharding import PartitionSpec as P

HD = 128
BLK = 64
VB = 64
HALF = 128
NY = 4
NZ = 16
NC = 2
GROUP = 4
NEG = -1e30
SCALE = HD**-0.5 * math.log2(math.e)
MESH = pl.DeviceIdType.MESH


TREE = {0: ((2, 2), (1, 1)), 2: ((2, 4), (1, 3)), 4: ((2, 6), (1, 5)), 6: ((2, 8), (1, 7))}
HOPS = (2, 1)
PAIRS = (1, 2, 3, 4, 5, 6)
LAST = 7
FIRST = (("own", 1), ("own", 2), ("first", 0))
EARLY = (("rest", 1), ("own", 4), ("own", 3), ("rest", 2))
STEPS = {
    1: (("own", 6), ("own", 5)),
    2: (("rest", 4),),
    3: (("rest", 3),),
    4: (("own", 8), ("own", 7)),
    5: (("rest", 6),),
    6: (("rest", 5),),
    8: (("rest", 8),),
    9: (("rest", 7),),
}
ROWS = 2 * VB
SPLIT = 64


def kernel(
    q_hbm, k_hbm, v_hbm, vr_hbm, slash_ref, bm_ref, out_hbm,
    q_ref, k_ref, v_ref, vr_ref, lines, bias_ref, peak, acc, res,
    in_sem, a_send, a_recv, b_send, b_recv, y_send, y_recv,
    s_send, s_recv, x_send, x_recv, own_sem,
):
    c = lax.axis_index("ctx")
    h = lax.axis_index("head")
    heads = lax.axis_size("head")
    y = c // (NZ * NC)
    z = (c // NC) % NZ
    core = c % NC

    def dev(yy, zz, cc):
        return (yy * (NZ * NC) + zz * NC + cc, h)

    sibling = dev(y, z, 1 - core)
    opposite = (y + 2) % NY

    def along(hop, upward):
        return (z + hop) % NZ if upward else (z + NZ - hop) % NZ

    def owner_of(distance, upward):
        return along(distance, not upward)

    loads = [
        pltpu.make_async_copy(src, dst, in_sem.at[i])
        for i, (src, dst) in enumerate(
            [(vr_hbm, vr_ref), (k_hbm, k_ref), (v_hbm, v_ref)]
            + [
                (
                    q_hbm.at[pl.ds(half * HALF, HALF), pl.ds(g * HD, HD)],
                    q_ref.at[half * GROUP + g],
                )
                for half in range(2)
                for g in range(GROUP)
            ]
        )
    ]
    for load in loads:
        load.start()

    barrier = pltpu.get_barrier_semaphore()
    greeted = [dev(y, along(hop, up), core) for hop in HOPS for up in (True, False)]
    greeted += [dev((y + d) % NY, z, core) for d in (1, 2, 3)]
    greeted += [(c, (h + d) % heads) for d in (1, 2, 3)]
    greeted += [sibling]
    for who in greeted:
        pl.semaphore_signal(barrier, inc=1, device_id=who, device_id_type=MESH)

    for load in loads[:3]:
        load.wait()
    chip_rows = vr_ref[y, pl.ds(z, 1), :]
    picks = lax.broadcasted_iota(jnp.int32, (2 * HALF, NC * VB), 0) == chip_rows
    picks = jnp.where(picks, 1.0, 0.0).astype(jnp.bfloat16)
    for kv, src in ((0, k_ref), (1, v_ref)):
        both = lax.dot_general(
            picks, src[...], (((0,), (0,)), ((), ())), preferred_element_type=jnp.float32
        ).astype(jnp.bfloat16)
        for cc in range(NC):
            @pl.when(core == cc)
            def _():
                lines[z, y, cc, kv * VB : (kv + 1) * VB] = both[cc * VB : (cc + 1) * VB]

    pl.semaphore_wait(barrier, len(greeted))

    def remote(block, send, recv, to):
        return pltpu.make_async_remote_copy(
            block, block, send, recv, device_id=to, device_id_type=MESH
        )

    def z_copy(kind, held, hop, reached, upward):
        zz = owner_of(held, upward)
        send, recv, yy, first = (
            (a_send, a_recv, y, 0) if kind == "own" else (b_send, b_recv, opposite, SPLIT)
        )
        cut = 64 if kind == "own" else 96
        last = ROWS
        if reached == 8:
            first, last = (first, cut) if upward else (cut, ROWS)
        return remote(
            lines.at[zz, yy, core, pl.ds(first, last - first)],
            send.at[int(upward), reached], recv.at[int(upward), reached],
            dev(y, along(hop, upward), core),
        )

    def z_sends(kind, held):
        return [
            z_copy(kind, held, hop, reached, upward)
            for hop, reached in TREE.get(held, ())
            for upward in (True, False)
        ]

    def z_arrivals(kind, reached):
        hop, held = next(
            (hop, held) for held, to in TREE.items() for hop, at in to if at == reached
        )
        return [z_copy(kind, held, hop, reached, upward) for upward in (True, False)]

    def y_copy(distance, d):
        rows = SPLIT if d == 2 and distance != 0 else ROWS
        return remote(
            lines.at[(z + NZ + distance) % NZ, y, core, pl.ds(0, rows)],
            y_send.at[d - 1, distance % NZ], y_recv.at[d - 1, distance % NZ],
            dev((y + d) % NY, z, core),
        )

    def s_copy(rel):
        return remote(
            lines.at[(z + rel) % NZ, :, core], s_send.at[rel], s_recv.at[rel], sibling
        )

    def signed(distance):
        return (0,) if distance == 0 else (8,) if distance == 8 else (-distance, distance)

    def own_step(distance):
        for copy in z_arrivals("own", distance):
            copy.wait_recv()
        for copy in z_sends("own", distance):
            copy.start()
        for at in signed(distance):
            for d in (2, 1, 3):
                y_copy(at, d).start()

    def rest_step(distance):
        for copy in z_arrivals("rest", distance):
            copy.wait_recv()
        for copy in z_sends("rest", distance):
            copy.start()
        for at in signed(distance):
            for d in (1, 2, 3):
                y_copy(at, d).wait_recv()
            s_copy(at % NZ).start()

    for copy in z_sends("own", 0):
        copy.start()
    for d in (2, 1, 3):
        y_copy(0, d).start()

    ones = jnp.ones((NY * NC * VB, HD), jnp.bfloat16)

    owner = (
        lax.broadcasted_iota(jnp.int32, (NZ, NC * VB), 0) * NC
        + lax.broadcasted_iota(jnp.int32, (NZ, NC * VB), 1) // VB
    )
    for yy in range(NY):
        is_low = vr_ref[yy] < HALF
        at = slice(yy * NC * VB, (yy + 1) * NC * VB)
        before = owner + yy * (NZ * NC) < c
        after = owner + yy * (NZ * NC) > c
        bias_ref[0, :, at] = jnp.where(is_low & before, 0.0, NEG)
        bias_ref[1, :, at] = jnp.where(is_low | after, 0.0, NEG)

    for load in loads[3:]:
        load.wait()

    qi = lax.broadcasted_iota(jnp.int32, (HALF, HALF), 0)
    kj = lax.broadcasted_iota(jnp.int32, (HALF, HALF), 1)
    offset = qi - kj
    slash_hit = offset == slash_ref[0]
    for n in range(1, slash_ref.shape[0]):
        slash_hit = slash_hit | (offset == slash_ref[n])
    base = (qi // BLK == kj // BLK) | slash_hit
    for half in range(2):
        bits = [
            [jnp.full((HALF, HALF), bm_ref[kb, 2 * half + qb], jnp.int32) for kb in range(2)]
            for qb in range(2)
        ]
        top = jnp.where(kj < BLK, bits[0][0], bits[0][1])
        low = jnp.where(kj < BLK, bits[1][0], bits[1][1])
        hit = jnp.where(qi < BLK, top, low) == 1
        allowed = (kj <= qi) & (base | hit)
        bias = jnp.where(allowed, 0.0, NEG)
        rows = slice(half * HALF, (half + 1) * HALF)
        vals = jnp.concatenate([v_ref[rows, :], ones[:HALF]], axis=1)
        for t in range(half * GROUP, (half + 1) * GROUP):
            s = lax.dot_general(
                q_ref[t], k_ref[rows, :], (((1,), (1,)), ((), ())),
                preferred_element_type=jnp.float32,
            )
            s = s + bias
            top_score = jnp.broadcast_to(jnp.max(s, axis=1, keepdims=True), s.shape)
            peak[t] = top_score
            weights = jnp.exp2((s - top_score) * SCALE).astype(jnp.bfloat16)
            acc[t] = jnp.dot(weights, vals, preferred_element_type=jnp.float32)

    def absorb(half, chunks):
        def all_keys(first):
            return jnp.concatenate(
                [lines[zz, :, :, first : first + VB].reshape(NY * NC * VB, HD) for zz in chunks],
                axis=0,
            )

        keys = all_keys(0)
        vals = jnp.concatenate(
            [all_keys(VB), jnp.concatenate([ones] * len(chunks), axis=0)], axis=1
        )
        bias = jnp.concatenate([bias_ref[half, pl.ds(zz, 1), :] for zz in chunks], axis=1)
        scores = [
            lax.dot_general(
                q_ref[half * GROUP + g], keys, (((1,), (1,)), ((), ())),
                preferred_element_type=jnp.float32,
            )
            + bias
            for g in range(GROUP)
        ]
        for g in range(GROUP):
            t = half * GROUP + g
            s = scores[g]
            old = peak[t]
            new = jnp.maximum(old, jnp.max(s, axis=1, keepdims=True))
            peak[t] = new
            weights = jnp.exp2((s - jnp.concatenate([new] * (NY * len(chunks)), axis=1)) * SCALE)
            rescale = jnp.exp2((old - new) * SCALE)
            acc[t] = acc[t] * jnp.concatenate([rescale] * 2, axis=1) + jnp.dot(
                weights.astype(jnp.bfloat16), vals, preferred_element_type=jnp.float32
            )

    def first_step(distance):
        for d in (2, 1, 3):
            y_copy(distance, d).wait_recv()
        for copy in z_sends("rest", distance):
            copy.start()
        s_copy(distance).start()

    def do(todo):
        for kind, distance in todo:
            {"own": own_step, "rest": rest_step, "first": first_step}[kind](distance)

    do(FIRST)

    def near(half, carry):
        absorb(half, [z])
        return carry

    s_copy(0).wait_recv()
    lax.fori_loop(0, 2, near, 0)

    do(EARLY)

    def pair(u, carry):
        half = u % 2
        for j, todo in STEPS.items():
            @pl.when(u == j)
            def _():
                do(todo)
        distance = jnp.int32(0)
        for j, at in enumerate(PAIRS):
            distance = jnp.where(u // 2 == j, at, distance)

        @pl.when(half == 0)
        def _():
            s_copy(NZ - distance).wait_recv()
            s_copy(distance).wait_recv()

        chunks = [(z + NZ - distance) % NZ, (z + distance) % NZ]

        @pl.when((half == 1) | (jnp.minimum(chunks[0], chunks[1]) * NC < c))
        def _():
            absorb(half, chunks)
        return carry

    lax.fori_loop(0, 2 * len(PAIRS), pair, 0)
    for rel in (NZ - LAST, LAST, 8):
        s_copy(rel).wait_recv()

    quarter = res.shape[0] // 4
    cols = GROUP * HD

    def x_copy(to, whose):
        return pltpu.make_async_remote_copy(
            res.at[pl.ds(to * quarter, quarter), :],
            out_hbm.at[:, pl.ds(pl.multiple_of(h * cols, cols), cols)],
            x_send.at[to], x_recv.at[whose],
            device_id=(c, to), device_id_type=MESH,
        )

    own = pltpu.make_async_copy(
        res.at[pl.ds(h * quarter, quarter), :],
        out_hbm.at[:, pl.ds(pl.multiple_of(h * cols, cols), cols)],
        own_sem,
    )

    def finish(half, carry):
        absorb(half, [(z + rel) % NZ for rel in (NZ - LAST, LAST, 8)])
        rows = pl.ds(pl.multiple_of(half * HALF, HALF), HALF)
        for g in range(GROUP):
            total = acc[half * GROUP + g]
            res[rows, g * HD : (g + 1) * HD] = (total[:, :HD] / total[:, HD:]).astype(jnp.bfloat16)
        for part in range(2):
            to = half * 2 + part
            @pl.when(to == h)
            def _():
                own.start()
            @pl.when(to != h)
            def _():
                x_copy(to, h).start()
        return carry

    lax.fori_loop(0, 2, finish, 0)

    for kind in ("own", "rest"):
        for held in TREE:
            for copy in z_sends(kind, held):
                copy.wait_send()
    for distance in range(NZ):
        for d in (1, 2, 3):
            y_copy(distance, d).wait_send()

    def drain(rel, carry):
        s_copy(rel).wait_send()
        return carry

    lax.fori_loop(0, NZ, drain, 0)
    own.wait()
    for to in range(4):
        @pl.when(to != h)
        def _():
            x_copy(to, to).wait_send()
            x_copy(to, to).wait_recv()


def on_device(queries, key_rows, value_rows, vertical_rows, slash_offsets, block_mask):
    rows = queries.shape[0]
    heads = lax.axis_size("head")
    cols = queries.shape[1]
    dma = pltpu.SemaphoreType.DMA
    return pl.pallas_call(
        kernel,
        out_shape=jax.ShapeDtypeStruct((rows // heads, heads * cols), jnp.bfloat16),
        in_specs=[pl.BlockSpec(memory_space=pltpu.HBM)] * 4
        + [pl.BlockSpec(memory_space=pltpu.SMEM)] * 2,
        out_specs=pl.BlockSpec(memory_space=pl.ANY),
        scratch_shapes=[
            pltpu.VMEM((2 * GROUP, HALF, HD), jnp.bfloat16),
            pltpu.VMEM((rows, HD), jnp.bfloat16),
            pltpu.VMEM((rows, HD), jnp.bfloat16),
            pltpu.VMEM((NY, NZ, NC * VB), jnp.int32),
            pltpu.VMEM((NZ, NY, NC, ROWS, HD), jnp.bfloat16),
            pltpu.VMEM((2, NZ, NY * NC * VB), jnp.float32),
            pltpu.VMEM((2 * GROUP, HALF, HD), jnp.float32),
            pltpu.VMEM((2 * GROUP, HALF, 2 * HD), jnp.float32),
            pltpu.VMEM((rows, cols), jnp.bfloat16),
            dma((3 + 2 * GROUP,)),
            dma((2, 9)), dma((2, 9)), dma((2, 9)), dma((2, 9)),
            dma((3, NZ)), dma((3, NZ)),
            dma((NZ,)), dma((NZ,)),
            dma((4,)), dma((4,)),
            dma,
        ],
        compiler_params=pltpu.CompilerParams(
            collective_id=0, has_side_effects=True, vmem_limit_bytes=60 * 1024 * 1024
        ),
        cost_estimate=pl.CostEstimate(
            flops=4 * 1024 * 8192 * HD, bytes_accessed=2**20, transcendentals=1024 * 8192
        ),
    )(
        queries, key_rows, value_rows,
        vertical_rows.reshape(NY, NZ, NC * VB),
        slash_offsets.reshape(-1),
        jnp.transpose(block_mask, (1, 2, 0)).reshape(2, -1),
    )


def solution(mesh):
    placed = (
        P("ctx", "head"),
        P("ctx", "head"),
        P("ctx", "head"),
        P(None, "head"),
        P(None, "head"),
        P("ctx", None, "head"),
    )
    return jax.shard_map(
        on_device, mesh=mesh, in_specs=placed, out_specs=P(("ctx", "head"), None), check_vma=False
    )
```
